32 devices in a mesh: sector: 2 (over y), rd: 4 (over x, core), pr: 4 (over z).
Axes of the slice: x: 2, y: 2, z: 4, core: 2. Of those that a mesh axis runs over, the one named last changes fastest.
Arguments:
- reading_geo: float32 [3, 131072], P(None, ('sector', 'rd')), parts along dimension 1, may hold values from 0 to 10, as said below
- prism_geo: float32 [3, 524288], P(None, ('sector', 'pr')), parts along dimension 1, may hold values from 0 to 10, as said below
- observed: float32 [131072], P(('sector', 'rd', 'pr')), parts along dimension 0, may hold values from -6 to 6
- warm_start: float32 [524288], P(('sector', 'pr', 'rd')), parts along dimension 0, may hold values from -6 to 6
- damping: float32 [524288], P(('sector', 'pr', 'rd')), parts along dimension 0, may hold values from 0.1 to 2
- pair_blocks: int32 [8, 4, 20, 2], P(('sector', 'rd'), 'pr'), parts along dimension 0, may hold values from 0 to 127, as said below
- pair_count: int32 [8, 4], P(('sector', 'rd'), 'pr'), parts along dimension 0, may hold values from 1 to 20, as said below
Outputs:
- solution: float32 [524288], P(('sector', 'pr', 'rd')), parts along dimension 0
- normal_residual: float32 [524288], P(('sector', 'pr', 'rd')), parts along dimension 0
The draws below stay inside these ranges and needn't reach their ends.
There are 2 independent parts, one for each index of `sector`. The reference program is written for one: setup_inputs(seed, part) draws one part's arguments, and reference() takes and returns one part's arrays. A program takes and returns all parts, laid end to end along the dimension named above; each array names one. Nothing has to cross between parts.
Inputs may be any that keep to these rules, and one draw needn't show every extreme that they name: `pair_blocks`: column 0 is a reading block of the device's rd row (0 to 31), column 1 a prism block of its pr column (0 to 127); the used slots of one device name distinct pairs; slots at or beyond pair_count are ignored. Taking the prism blocks in aligned runs of 32, the slots of one device name at most 2 distinct prism blocks of any one run, and the first 2 slots of every device name 2 distinct blocks of one run. `pair_count`: one device of the sector uses all 20 slots. `reading_geo`: Rows: east and north within 0 to 10, height 0.3 to 0.6. `prism_geo`: Rows: east and north within 0 to 10, depth 1 to 2.
All inputs are finite; a program needn't handle non-finite values.
Results may differ from the reference program's by a relative error of at most 0.0003.
Values sent between devices are 32-bit elements; how exact they have to be, the bound alone decides.
No kernel may reach another device: no remote copies, remote signals or barrier semaphores. Data moves between devices by JAX's collectives and lax.ppermute only.
A program may use at most 64 MiB of HBM per device.

```python
import math
import jax
import jax.numpy as jnp
from jax import lax

BLK = 512
SLOTS = 2
RBLK = 32
PBLK = 128
CAP = 20
ITERS = 2
NR = 65536
NP = 262144
N_RD = 4
N_PR = 4


box_km = 10.0


def draw_reading_geo(key, part):
    key = jax.random.fold_in(key, 1)
    keys = jax.random.split(key, 3)
    east = box_km * jax.random.uniform(keys[0], (NR,), jnp.float32)
    north = box_km * jax.random.uniform(keys[1], (NR,), jnp.float32)
    height = 0.3 + 0.3 * jax.random.uniform(keys[2], (NR,), jnp.float32)
    return jnp.stack([east, north, height]).astype(jnp.float32)


def draw_prism_geo(key, part):
    key = jax.random.fold_in(key, 2)
    keys = jax.random.split(key, 3)
    east = box_km * jax.random.uniform(keys[0], (NP,), jnp.float32)
    north = box_km * jax.random.uniform(keys[1], (NP,), jnp.float32)
    depth = 1.0 + jax.random.uniform(keys[2], (NP,), jnp.float32)
    return jnp.stack([east, north, depth]).astype(jnp.float32)


def device_pairs(sub):
    share_blocks = PBLK // N_RD
    lanes = N_RD * SLOTS
    combos = RBLK * lanes
    keys = jax.random.split(sub, 4)
    allowed = jax.vmap(lambda one_key: jax.random.permutation(one_key, share_blocks)[:SLOTS])(jax.random.split(keys[0], N_RD)).astype(jnp.int32)
    pinned_row = jax.random.randint(keys[1], (), 0, RBLK)
    pinned_share = jax.random.randint(keys[2], (), 0, N_RD)
    pinned = (pinned_row * lanes + pinned_share * SLOTS + jnp.arange(SLOTS, dtype=jnp.int32)).astype(jnp.int32)
    order = jax.random.permutation(keys[3], combos).astype(jnp.int32)
    clash = jnp.any(order[:, None] == pinned[None, :], axis=1).astype(jnp.int32)
    rest = order[jnp.argsort(clash, stable=True)]
    chosen = jnp.concatenate([pinned, rest[:CAP - SLOTS]]).astype(jnp.int32)
    reading = chosen // lanes
    lane = chosen % lanes
    share = lane // SLOTS
    slot = lane % SLOTS
    prism = share * share_blocks + allowed[share, slot]
    return jnp.stack([reading, prism], axis=-1).astype(jnp.int32)


def draw_pair_blocks(key, part):
    key = jax.random.fold_in(key, 3)
    keys = jax.random.split(key, N_RD * N_PR)
    pairs = jax.vmap(device_pairs)(keys)
    return pairs.reshape(N_RD, N_PR, CAP, 2).astype(jnp.int32)


def draw_pair_count(key, part):
    key = jax.random.fold_in(key, 4)
    keys = jax.random.split(key, 3)
    first = jax.random.randint(keys[0], (N_RD * N_PR,), 1, CAP + 1)
    second = jax.random.randint(keys[1], (N_RD * N_PR,), 1, CAP + 1)
    counts = jnp.maximum(first * second // CAP, 1)
    busiest = jax.random.randint(keys[2], (), 0, N_RD * N_PR)
    counts = jnp.where(jnp.arange(N_RD * N_PR) == busiest, CAP, counts)
    return counts.reshape(N_RD, N_PR).astype(jnp.int32)


def steps_of(own_key, shape, cuts, low, high):
    level, own = 1.0, jax.random.fold_in(own_key, 6)
    for dim, parts in cuts:
        heights = jnp.exp(jax.random.uniform(jax.random.fold_in(own, dim), (parts,), jnp.float32, low / len(cuts), high / len(cuts)))
        level = level * jnp.repeat(heights, shape[dim] // parts).reshape([-1 if axis == dim else 1 for axis in range(len(shape))])
    return level


def centred(own_key, extent, deviation, most, shards=(), kind=jnp.bfloat16):
    values = deviation * jax.random.normal(own_key, extent, jnp.float32)
    if shards:
        values = values * steps_of(own_key, extent, shards, -0.22, 0.18)
    return jnp.clip(values, -most, most).astype(kind)


def setup_inputs(seed: int = 0, part: int = 0) -> dict:
    seeds = jax.random.split(jax.random.key(seed), 8)
    part_keys = jax.random.split(jax.random.fold_in(seeds[7], part), 8)
    reading_geo = draw_reading_geo(jax.random.fold_in(jax.random.fold_in(seeds[7], part), 71), part)
    prism_geo = draw_prism_geo(jax.random.fold_in(jax.random.fold_in(seeds[7], part), 71), part)
    observed = centred(part_keys[2], (NR,), 1.0, 6.0, ((0, 16),), jnp.float32)
    warm_start = centred(part_keys[3], (NP,), 1.0, 6.0, ((0, 16),), jnp.float32)
    damping = jnp.clip(jnp.exp(math.log(2.0) - 2.9957323 * jax.random.uniform(part_keys[4], (NP,), jnp.float32) ** steps_of(part_keys[4], (NP,), ((0, 16),), -0.2, 0.2)), 0.1, 2.0)
    pair_blocks = draw_pair_blocks(jax.random.fold_in(jax.random.fold_in(seeds[7], part), 71), part)
    pair_count = draw_pair_count(jax.random.fold_in(jax.random.fold_in(seeds[7], part), 71), part)
    return {"reading_geo": reading_geo, "prism_geo": prism_geo, "observed": observed, "warm_start": warm_start, "damping": damping, "pair_blocks": pair_blocks, "pair_count": pair_count}


kernel_scale = 0.125

def kernel_tile(reading_geo, prism_geo, reading_start, prism_start):
    readings = lax.dynamic_slice_in_dim(reading_geo, reading_start, BLK, 1)
    prisms = lax.dynamic_slice_in_dim(prism_geo, prism_start, BLK, 1)
    east = readings[0][:, None] - prisms[0][None, :]
    north = readings[1][:, None] - prisms[1][None, :]
    vertical = readings[2][:, None] + prisms[2][None, :]
    squared = east * east + north * north + vertical * vertical
    return kernel_scale * vertical / (squared * jnp.sqrt(squared))

def reference(reading_geo, prism_geo, observed, warm_start, damping, pair_blocks, pair_count):
    row_base = (jnp.arange(N_RD, dtype=jnp.int32) * RBLK)[:, None, None]
    column_base = (jnp.arange(N_PR, dtype=jnp.int32) * PBLK)[None, :, None]
    reading_blocks = (pair_blocks[..., 0].astype(jnp.int32) + row_base).reshape(-1)
    prism_blocks = (pair_blocks[..., 1].astype(jnp.int32) + column_base).reshape(-1)
    live = (jnp.arange(CAP, dtype=jnp.int32)[None, None, :] < pair_count[:, :, None].astype(jnp.int32)).reshape(-1)
    order = jnp.argsort(jnp.where(live, 0, 1).astype(jnp.int32), stable=True)
    reading_blocks = reading_blocks[order]
    prism_blocks = prism_blocks[order]
    live_total = jnp.sum(live.astype(jnp.int32))

    def forward(values):

        def advance(position, totals):
            row_start = (reading_blocks[position] * BLK).astype(jnp.int32)
            col_start = (prism_blocks[position] * BLK).astype(jnp.int32)
            tile = kernel_tile(reading_geo, prism_geo, row_start, col_start)
            piece = lax.dynamic_slice_in_dim(values, col_start, BLK)
            added = jnp.dot(tile, piece, precision=lax.Precision.HIGHEST)
            current = lax.dynamic_slice_in_dim(totals, row_start, BLK)
            return lax.dynamic_update_slice_in_dim(totals, current + added, row_start, 0)
        return lax.fori_loop(0, live_total, advance, jnp.zeros((NR,), jnp.float32))

    def adjoint(values):

        def advance(position, totals):
            row_start = (reading_blocks[position] * BLK).astype(jnp.int32)
            col_start = (prism_blocks[position] * BLK).astype(jnp.int32)
            tile = kernel_tile(reading_geo, prism_geo, row_start, col_start)
            piece = lax.dynamic_slice_in_dim(values, row_start, BLK)
            added = jnp.dot(piece, tile, precision=lax.Precision.HIGHEST)
            current = lax.dynamic_slice_in_dim(totals, col_start, BLK)
            return lax.dynamic_update_slice_in_dim(totals, current + added, col_start, 0)
        return lax.fori_loop(0, live_total, advance, jnp.zeros((NP,), jnp.float32))
    solution = warm_start
    misfit = observed - forward(solution)
    normal_residual = adjoint(misfit) - damping * solution
    direction = normal_residual
    norm_now = jnp.sum(normal_residual * normal_residual)
    for iteration in range(ITERS):
        image = forward(direction)
        product = adjoint(image) + damping * direction
        step_length = norm_now / jnp.sum(direction * product)
        solution = solution + step_length * direction
        normal_residual = normal_residual - step_length * product
        norm_next = jnp.sum(normal_residual * normal_residual)
        direction = normal_residual + norm_next / norm_now * direction
        norm_now = norm_next
    return (solution, normal_residual)
```

```python
import functools

import jax
import jax.numpy as jnp
from jax import lax
from jax.experimental import pallas as pl
from jax.experimental.pallas import tpu as pltpu
from jax.sharding import PartitionSpec as P

BLK = 512
LANES = 128
HALF = LANES // 2
ROWS = BLK // LANES
GROUPS = BLK // 8
SLOTS = 2
VMEM_LIMIT = 12 * 1024 * 1024

length_scale = 8.0**0.5

F32 = jnp.float32
VMEM = pltpu.VMEM
SMEM = pltpu.SMEM


def call(kernel, name, outs, ins, args, scratch=()):
    return pl.pallas_call(
        kernel,
        name=name,
        out_shape=outs,
        in_specs=[pl.BlockSpec(memory_space=s) for s in ins],
        out_specs=[pl.BlockSpec(memory_space=o.memory_space) for o in outs],
        scratch_shapes=scratch,
        compiler_params=pltpu.CompilerParams(vmem_limit_bytes=VMEM_LIMIT),
    )(*args)


def lane_index(shape):
    return lax.broadcasted_iota(jnp.int32, shape, len(shape) - 1)


def spread(block):
    return jnp.concatenate([block, pltpu.roll(block, HALF, 1)], axis=0)


def gather_back(res):
    return res[0:ROWS] + pltpu.roll(res[ROWS:], HALF, 1)


def total(values):
    return jnp.sum(jnp.sum(values, axis=0), keepdims=True)


def prep_kernel(pairs, count, x0, damp, payload, table, ids):
    own = x0.shape[0]
    slots = ids.shape[0]
    for s in range(slots):
        ids[s] = -1

    def assign(i, carry):
        block = pairs[i, 1]
        share = block // own
        held = ids[share * SLOTS]
        here = jnp.logical_or(held < 0, held == block)
        slot = share * SLOTS + jnp.where(here, 0, 1)
        ids[slot] = block
        table[0, i] = pairs[i, 0]
        table[1, i] = slot
        return carry

    lax.fori_loop(0, count[0, 0], assign, 0)
    payload[0:own] = x0[...]
    payload[own : 2 * own] = damp[...]
    for s in range(slots):
        payload[2 * own + s] = jnp.full((ROWS, LANES), ids[s].astype(F32))


def tiles_kernel(table, ids, count, readings, prisms, tiles):
    def one(i, carry):
        a = table[0, i]
        b = ids[table[1, i]]
        rgeo = readings[:, pl.ds(pl.multiple_of(a * BLK, BLK), BLK)] * length_scale
        pgeo = prisms[:, pl.ds(pl.multiple_of(b * BLK, BLK), BLK)] * length_scale

        def column(k):
            return spread(
                jnp.concatenate([pgeo[k : k + 1, q * LANES : (q + 1) * LANES] for q in range(ROWS)], axis=0)
            )

        east, north, depth = (column(k) for k in range(3))
        chunk = [
            [jnp.broadcast_to(rgeo[k : k + 1, c * LANES : (c + 1) * LANES], (8, LANES)) for c in range(ROWS)]
            for k in range(3)
        ]
        for v in range(GROUPS):
            pe = jnp.broadcast_to(east[:, v : v + 1], (8, LANES))
            pn = jnp.broadcast_to(north[:, v : v + 1], (8, LANES))
            pd = jnp.broadcast_to(depth[:, v : v + 1], (8, LANES))
            for c in range(ROWS):
                e = chunk[0][c] - pe
                n = chunk[1][c] - pn
                w = chunk[2][c] + pd
                inv = lax.rsqrt(e * e + n * n + w * w)
                tiles[i * GROUPS + v, :, c * LANES : (c + 1) * LANES] = (w * inv) * (inv * inv)
        return carry

    lax.fori_loop(0, count[0, 0], one, 0)


def forward_tiles(table, count, tiles, need, out):
    def one(i, carry):
        a = table[0, i]
        s = table[1, i]
        values = spread(need[s])
        sums = [[jnp.zeros((8, LANES), F32) for _ in range(ROWS)] for _ in range(2)]
        for v in range(GROUPS):
            pb = jnp.broadcast_to(values[:, v : v + 1], (8, LANES))
            for c in range(ROWS):
                sums[v % 2][c] += tiles[i * GROUPS + v, :, c * LANES : (c + 1) * LANES] * pb
        added = [jnp.sum(sums[0][c] + sums[1][c], axis=0, keepdims=True) for c in range(ROWS)]
        out[a] += jnp.concatenate(added, axis=0)
        return carry

    lax.fori_loop(0, count[0, 0], one, 0)


def adjoint_tiles(table, count, tiles, row, out):
    lane = lane_index((8, LANES))

    def one(i, carry):
        a = table[0, i]
        s = table[1, i]
        values = row[a]
        yb = [jnp.broadcast_to(values[c : c + 1], (8, LANES)) for c in range(ROWS)]
        res = jnp.zeros((8, LANES), F32)
        for v in range(GROUPS):
            t = [tiles[i * GROUPS + v, :, c * LANES : (c + 1) * LANES] * yb[c] for c in range(ROWS)]
            r = jnp.sum((t[0] + t[1]) + (t[2] + t[3]), axis=1, keepdims=True)
            res = jnp.where(lane == v, r, res)
        out[s] += gather_back(res)
        return carry

    lax.fori_loop(0, count[0, 0], one, 0)


def scalar_tile(values):
    lane = lane_index((ROWS, LANES))
    row = lax.broadcasted_iota(jnp.int32, (ROWS, LANES), 0)
    tile = jnp.zeros((ROWS, LANES), F32)
    for k, value in enumerate(values):
        tile = jnp.where(jnp.logical_and(lane == k, row == 0), value, tile)
    return tile


def first_forward_kernel(n_rd, *refs):
    where_am_i, table, ids, count, obs, tiles = refs[:6]
    sent = refs[6 : 6 + n_rd]
    out, x0n, dampn, names = refs[6 + n_rd :]
    slots = ids.shape[0]
    own = (sent[0].shape[0] - slots) // 2
    me = where_am_i[0]
    for k in range(n_rd):
        share = partner(me, k, n_rd)
        for j in range(SLOTS):
            slot = share * SLOTS + j
            local = jnp.maximum(ids[slot] - share * own, 0)
            x0n[slot] = sent[k][local]
            dampn[slot] = sent[k][own + local]
        names[k] = sent[k][2 * own : 2 * own + slots]
    out[...] = jnp.zeros(out.shape, F32)
    forward_tiles(table, count, tiles, x0n, out)
    out[...] = -out[...]
    mine = obs.shape[0]
    start = where_am_i[1] * mine
    out[pl.ds(start, mine)] = out[pl.ds(start, mine)] + obs[...]


def row_kernel(n_pr, stage, *refs):
    table, count, tiles = refs[:3]
    shares = refs[3 : 3 + n_pr]
    rest = refs[3 + n_pr :]
    if stage == 2:
        image0, rest = rest[0], rest[1:]
    payload, image = rest[:2]
    blocks = image.shape[0]
    slots = payload.shape[0] - 1
    summed = shares[0][0:blocks]
    for share in shares[1:]:
        summed = summed + share[0:blocks]
    image[...] = summed
    payload[...] = jnp.zeros(payload.shape, F32)
    if stage > 0:
        scalars = shares[0][blocks]
        for share in shares[1:]:
            scalars = scalars + share[blocks]
        added = [0.0, total(summed * summed)]
        if stage == 2:
            added.append(total(summed * image0[...]))
        payload[slots] = scalars + scalar_tile(added)
    adjoint_tiles(table, count, tiles, image, payload)


def own_sums(me, names, sent, own):
    blocks = [jnp.zeros((ROWS, LANES), F32) for _ in range(own)]
    for k in range(len(sent)):
        for j in range(SLOTS):
            slot = me * SLOTS + j
            tag = names[k, slot]
            values = sent[k][slot]
            for b in range(own):
                blocks[b] = blocks[b] + jnp.where(tag == (me * own + b).astype(F32), values, 0.0)
    return jnp.stack(blocks)


def needed_sums(names, sent, slots):
    found = []
    for s in range(slots):
        tag = names[0, s]
        value = sent[0][s]
        for k in range(1, len(sent)):
            for j in range(SLOTS):
                other = s // SLOTS * SLOTS + j
                value = value + jnp.where(names[k, other] == tag, sent[k][other], 0.0)
        found.append(value)
    return jnp.stack(found)


def second_forward_kernel(n_rd, *refs):
    where_am_i, table, count, tiles, names, x0, damp, x0n, dampn = refs[:9]
    sent = refs[9 : 9 + n_rd]
    out, res, resn = refs[9 + n_rd :]
    blocks = out.shape[0] - 1
    me = where_am_i[0]
    own = x0.shape[0]
    r = own_sums(me, names, sent, own) - damp[...] * x0[...]
    res[...] = r
    resn[...] = needed_sums(names, sent, resn.shape[0]) - dampn[...] * x0n[...]
    out[...] = jnp.zeros(out.shape, F32)
    out[blocks] = scalar_tile([total(r * r), total(damp[...] * r * r)])
    forward_tiles(table, count, tiles, resn, out)


def column_scalars(sent, slots, many):
    summed = sent[0][slots]
    for other in sent[1:]:
        summed = summed + other[slots]
    return [summed[0:1, k : k + 1] for k in range(many)]


def third_forward_kernel(n_rd, *refs):
    where_am_i, table, count, tiles, names, x0, damp, dampn, res0, res0n = refs[:10]
    sent = refs[10 : 10 + n_rd]
    out, x1, res1, prod0, known, res1n = refs[10 + n_rd :]
    blocks = out.shape[0] - 1
    slots = res0n.shape[0]
    me = where_am_i[0]
    own = x0.shape[0]
    r0 = res0[...]
    q0 = own_sums(me, names, sent, own) + damp[...] * r0
    norm, bending = column_scalars(sent, slots, 2)
    step = norm / bending
    prod0[...] = q0
    x1[...] = x0[...] + step * r0
    r1 = r0 - step * q0
    res1[...] = r1
    res1n[...] = res0n[...] - step * (needed_sums(names, sent, slots) + dampn[...] * res0n[...])
    known[0] = scalar_tile([norm, bending])
    out[...] = jnp.zeros(out.shape, F32)
    out[blocks] = scalar_tile([total(r1 * r1), total(damp[...] * r1 * r1), total(damp[...] * r1 * r0)])
    forward_tiles(table, count, tiles, res1n, out)


def last_kernel(n_rd, *refs):
    where_am_i, names, damp, x1, res0, res1, prod0, known = refs[:8]
    sent = refs[8 : 8 + n_rd]
    x2, res2 = refs[8 + n_rd :]
    me = where_am_i[0]
    own = damp.shape[0]
    slots = names.shape[1]
    r1 = res1[...]
    h1 = own_sums(me, names, sent, own) + damp[...] * r1
    norm1, r1_a_r1, r1_a_r0 = column_scalars(sent, slots, 3)
    norm0 = known[0][0:1, 0:1]
    bending0 = known[0][0:1, 1:2]
    ratio = norm1 / norm0
    bending = r1_a_r1 + ratio * (2.0 * r1_a_r0 + ratio * bending0)
    step = norm1 / bending
    x2[...] = x1[...] + step * (r1 + ratio * res0[...])
    res2[...] = r1 - step * (h1 + ratio * prod0[...])


def partner(me, k, n):
    if n & (n - 1) == 0:
        return me ^ k
    return lax.rem(me + n - k, n)


def exchange(values, axis, n):
    got = [values]
    for k in range(1, n):
        if n & (n - 1) == 0:
            pairs = [(i, i ^ k) for i in range(n)]
        else:
            pairs = [(i, (i + k) % n) for i in range(n)]
        got.append(lax.ppermute(values, axis, pairs))
    return got


def body(n_rd, n_pr, reading_geo, prism_geo, observed, warm_start, damping, pair_blocks, pair_count):
    cap = pair_blocks.shape[2]
    pairs = pair_blocks.reshape(cap, 2)
    own = warm_start.shape[0] // BLK
    rblk = reading_geo.shape[1] // BLK
    slots = n_rd * SLOTS
    shaped = lambda v: v.reshape(-1, ROWS, LANES)
    x0, damp, obs = shaped(warm_start), shaped(damping), shaped(observed)
    place = jnp.stack([lax.axis_index("rd"), lax.axis_index("pr")]).astype(jnp.int32)
    array = lambda *lead: VMEM((*lead, ROWS, LANES), F32)

    payload, table, ids = call(
        prep_kernel,
        "prep",
        [array(2 * own + slots), SMEM((2, cap), jnp.int32), SMEM((slots,), jnp.int32)],
        [SMEM, SMEM, VMEM, VMEM],
        [pairs, pair_count, x0, damp],
    )
    columns = exchange(payload, "rd", n_rd)
    (tiles,) = call(
        tiles_kernel,
        "tiles",
        [VMEM((cap * GROUPS, 8, BLK), F32)],
        [SMEM, SMEM, SMEM, VMEM, VMEM],
        [table, ids, pair_count, reading_geo, prism_geo],
    )
    share, x0n, dampn, names = call(
        functools.partial(first_forward_kernel, n_rd),
        "first_forward",
        [array(rblk), array(slots), array(slots), array(n_rd, slots)],
        [SMEM] * 4 + [VMEM] * (2 + n_rd),
        [place, table, ids, pair_count, obs, tiles, *columns],
    )
    rows = exchange(share, "pr", n_pr)

    def row_stage(stage, rows, extra):
        return call(
            functools.partial(row_kernel, n_pr, stage),
            f"row_{stage}",
            [array(slots + 1), array(rblk)],
            [SMEM] * 2 + [VMEM] * (1 + n_pr + len(extra)),
            [table, pair_count, tiles, *rows, *extra],
        )

    sums, _ = row_stage(0, rows, [])
    columns = exchange(sums, "rd", n_rd)
    share, res0, res0n = call(
        functools.partial(second_forward_kernel, n_rd),
        "second_forward",
        [array(rblk + 1), array(own), array(slots)],
        [SMEM] * 3 + [VMEM] * (6 + n_rd),
        [place, table, pair_count, tiles, names, x0, damp, x0n, dampn, *columns],
    )
    rows = exchange(share, "pr", n_pr)
    sums, image0 = row_stage(1, rows, [])
    columns = exchange(sums, "rd", n_rd)
    share, x1, res1, prod0, known, _ = call(
        functools.partial(third_forward_kernel, n_rd),
        "third_forward",
        [array(rblk + 1), array(own), array(own), array(own), array(1), array(slots)],
        [SMEM] * 3 + [VMEM] * (7 + n_rd),
        [place, table, pair_count, tiles, names, x0, damp, dampn, res0, res0n, *columns],
    )
    rows = exchange(share, "pr", n_pr)
    sums, _ = row_stage(2, rows, [image0])
    columns = exchange(sums, "rd", n_rd)
    x2, res2 = call(
        functools.partial(last_kernel, n_rd),
        "last",
        [array(own), array(own)],
        [SMEM] + [VMEM] * (7 + n_rd),
        [place, names, damp, x1, res0, res1, prod0, known, *columns],
    )
    return x2.reshape(-1), res2.reshape(-1)


def solution(mesh):
    placed = (
        P(None, ("sector", "rd")),
        P(None, ("sector", "pr")),
        P(("sector", "rd", "pr")),
        P(("sector", "pr", "rd")),
        P(("sector", "pr", "rd")),
        P(("sector", "rd"), "pr", None, None),
        P(("sector", "rd"), "pr"),
    )
    return jax.shard_map(
        functools.partial(body, mesh.shape["rd"], mesh.shape["pr"]),
        mesh=mesh,
        in_specs=placed,
        out_specs=(P(("sector", "pr", "rd")), P(("sector", "pr", "rd"))),
        check_vma=False,
    )
```

```python
import functools

import jax
import jax.numpy as jnp
from jax import lax
from jax.experimental import pallas as pl
from jax.experimental.pallas import tpu as pltpu
from jax.sharding import PartitionSpec as P

BLK = 512
LANES = 128
ROWS = BLK // LANES
GROUPS = BLK // 8
SLOTS = 2
MIB = 1024 * 1024
FEATURES = 64

length_scale = 8.0**0.5

F32 = jnp.float32
BF16 = jnp.bfloat16
I32 = jnp.int32
VMEM = pltpu.VMEM
SMEM = pltpu.SMEM


def call(kernel, name, room, outs, ins, args, scratch=()):
    return pl.pallas_call(
        kernel,
        name=name,
        out_shape=outs,
        in_specs=[pl.BlockSpec(memory_space=s) for s in ins],
        out_specs=[pl.BlockSpec(memory_space=getattr(o, "memory_space", VMEM)) for o in outs],
        scratch_shapes=scratch,
        compiler_params=pltpu.CompilerParams(vmem_limit_bytes=room * MIB),
    )(*args)


def lane_index(shape):
    return lax.broadcasted_iota(jnp.int32, shape, len(shape) - 1)


def each(count, one):
    lax.fori_loop(0, count, lambda i, carry: (one(i), carry)[1], 0)


def over(n, one, carry=0):
    if n > 8:
        return lax.fori_loop(0, n, one, carry)
    for s in range(n):
        carry = one(s, carry)
    return carry


def split3(x):
    a = x.astype(BF16).astype(F32)
    b = (x - a).astype(BF16).astype(F32)
    return a, b, x - a - b


def total(values):
    return jnp.sum(jnp.sum(values, axis=0), keepdims=True)


def prep_kernel(pairs, count, place, x0, damp, payload, table, ids, info, sems):
    own = x0.shape[0]
    slots = ids.shape[0]
    copies = [
        pltpu.make_async_copy(x0, payload.at[pl.ds(0, own)], sems.at[0]),
        pltpu.make_async_copy(damp, payload.at[pl.ds(own, own)], sems.at[1]),
    ]
    for copy in copies:
        copy.start()
    for s in range(slots):
        ids[s] = -1
    info[0] = place[0]
    info[1] = place[1]
    info[2] = count[0, 0]

    def assign(i, carry):
        block = pairs[1, i]
        share = block // own
        held = ids[share * SLOTS]
        here = jnp.logical_or(held < 0, held == block)
        slot = share * SLOTS + jnp.where(here, 0, 1)
        ids[slot] = block
        table[0, i] = pairs[0, i]
        table[1, i] = slot
        return carry

    lax.fori_loop(0, count[0, 0], assign, 0)
    payload[2 * own] = scalar_tile([ids[s].astype(F32) for s in range(slots)])
    for copy in copies:
        copy.wait()


def scaled(geo):
    row = lax.broadcasted_iota(I32, geo.shape, 0)
    return (geo - jnp.where(row < 2, 5.0, 0.0)) * length_scale


def features(geo, reading):
    row = lax.broadcasted_iota(I32, geo.shape, 0)
    norm = split3(jnp.broadcast_to(jnp.sum(geo * geo, axis=0, keepdims=True), geo.shape))
    last = jnp.where(row < 6, 1.0, 0.0)
    for k in range(3):
        last = jnp.where(row == (k if reading else 3 + k), norm[k], last)
    if reading:
        a, b, c = split3(geo * jnp.where(row < 2, -2.0, 2.0))
        blocks = [a, a, b, b, a, c, last]
    else:
        a, b, c = split3(geo)
        blocks = [a, b, a, b, c, a, last]
    blocks += [jnp.zeros_like(geo)] * (FEATURES // 8 - len(blocks))
    return jnp.concatenate(blocks, axis=0).astype(BF16)


def tiles_kernel(table, ids, info, readings, prisms, tiles, rgeo, pgeo, depth, feats, rsems, psems):
    slots = ids.shape[0]
    count = info[2]

    def reading_copy(i):
        start = pl.multiple_of(table[0, i] * BLK, BLK)
        return pltpu.make_async_copy(readings.at[:, pl.ds(start, BLK)], rgeo.at[i, pl.ds(0, 3)], rsems.at[i])

    def prism_copy(s):
        start = pl.multiple_of(jnp.maximum(ids[s], 0) * BLK, BLK)
        return pltpu.make_async_copy(prisms.at[:, pl.ds(start, BLK)], pgeo.at[s, pl.ds(0, 3)], psems.at[s])

    rgeo[...] = jnp.zeros(rgeo.shape, F32)
    pgeo[...] = jnp.zeros(pgeo.shape, F32)
    for s in range(slots):
        prism_copy(s).start()
    lax.fori_loop(0, count, lambda i, c: (reading_copy(i).start(), c)[1], 0)

    def prepare(s, carry):
        prism_copy(s).wait()
        geo = scaled(pgeo[s])
        feats[s] = features(geo, False).astype(F32)
        for q in range(ROWS):
            turned = geo[:, q * LANES : (q + 1) * LANES].T
            for g in range(GROUPS // ROWS):
                depth[s * GROUPS + q * (GROUPS // ROWS) + g] = jnp.broadcast_to(
                    turned[8 * g : 8 * g + 8, 2:3], (8, LANES)
                )
        return carry

    over(slots, prepare)
    lax.fori_loop(0, count, lambda i, c: (reading_copy(i).wait(), c)[1], 0)

    def one(i):
        s = table[1, i]
        geo = scaled(rgeo[i])
        mine = features(geo, True)
        theirs = feats[s].astype(BF16)
        tile = tiles.at[pl.ds(i * GROUPS, GROUPS)]
        depths = depth.at[pl.ds(s * GROUPS, GROUPS)]
        height = [jnp.broadcast_to(geo[2:3, c * LANES : (c + 1) * LANES], (8, LANES)) for c in range(ROWS)]
        for q in range(ROWS):
            squared = lax.dot_general(
                theirs[:, q * LANES : (q + 1) * LANES], mine, (((0,), (0,)), ((), ())), preferred_element_type=F32
            )
            for g in range(GROUPS // ROWS):
                v = q * (GROUPS // ROWS) + g
                up = depths[v]
                for c in range(ROWS):
                    w = height[c] + up
                    inv = lax.rsqrt(squared[8 * g : 8 * g + 8, c * LANES : (c + 1) * LANES])
                    tile[v, :, c * LANES : (c + 1) * LANES] = (w * inv) * (inv * inv)

    def two(i, carry):
        one(2 * i)
        one(jnp.minimum(2 * i + 1, count - 1))
        return carry

    lax.fori_loop(0, (count + 1) // 2, two, 0)


def spread_lanes(need, spread):
    slots = need.shape[0]
    values = need[...].reshape(slots * ROWS, LANES)
    left = jnp.concatenate(split3(values), axis=0).astype(BF16)
    shape = (3 * slots * ROWS, ROWS * LANES)
    row = lax.broadcasted_iota(I32, shape, 0) % (slots * ROWS)
    part = lax.broadcasted_iota(I32, shape, 1) // LANES

    def one(s, carry):
        pick = jnp.where(row == ROWS * s + part, 1.0, 0.0).astype(BF16)
        got = lax.dot_general(left, pick, (((0,), (0,)), ((), ())), preferred_element_type=F32)
        for q in range(ROWS):
            for g in range(GROUPS // ROWS):
                spread[s * GROUPS + q * (GROUPS // ROWS) + g] = got[8 * g : 8 * g + 8, q * LANES : (q + 1) * LANES]
        return carry

    over(slots, one)


def forward_tiles(table, count, tiles, need, spread, out):
    spread_lanes(need, spread)

    def one(i):
        a = table[0, i]
        s = table[1, i]
        tile = tiles.at[pl.ds(i * GROUPS, GROUPS)]
        column = spread.at[pl.ds(s * GROUPS, GROUPS)]
        sums = [[jnp.zeros((8, LANES), F32) for _ in range(ROWS)] for _ in range(2)]
        for v in range(GROUPS):
            values = column[v]
            for c in range(ROWS):
                sums[v % 2][c] += tile[v, :, c * LANES : (c + 1) * LANES] * values
        added = [jnp.sum(sums[0][c] + sums[1][c], axis=0, keepdims=True) for c in range(ROWS)]
        out[a] += jnp.concatenate(added, axis=0)

    each(count, one)


def adjoint_tiles(table, count, tiles, row, wide, out):
    slots = wide.shape[0] // GROUPS
    wide[...] = jnp.zeros(wide.shape, F32)

    def one(i):
        s = table[1, i]
        values = row[table[0, i]]
        spread = [jnp.broadcast_to(values[c : c + 1], (8, LANES)) for c in range(ROWS)]
        tile = tiles.at[pl.ds(i * GROUPS, GROUPS)]
        held = wide.at[pl.ds(s * GROUPS, GROUPS)]
        for v in range(GROUPS):
            t = [tile[v, :, c * LANES : (c + 1) * LANES] * spread[c] for c in range(ROWS)]
            held[v] += (t[0] + t[1]) + (t[2] + t[3])

    each(count, one)
    lane = lane_index((8, LANES))

    def reduce(s, groups):
        groups = list(groups)
        for g in range(GROUPS // ROWS):
            for q in range(ROWS):
                added = jnp.sum(wide[s * GROUPS + q * (GROUPS // ROWS) + g], axis=1, keepdims=True)
                groups[g] = jnp.where(lane == ROWS * s + q, added, groups[g])
        return tuple(groups)

    groups = over(slots, reduce, (jnp.zeros((8, LANES), F32),) * (GROUPS // ROWS))
    flat = jnp.concatenate(groups, axis=0).T
    out[0:slots] = flat[0 : slots * ROWS].reshape(slots, ROWS, LANES)


def scalar_tile(values):
    lane = lane_index((ROWS, LANES))
    row = lax.broadcasted_iota(I32, (ROWS, LANES), 0)
    tile = jnp.zeros((ROWS, LANES), F32)
    for k, value in enumerate(values):
        tile = jnp.where(jnp.logical_and(lane == k, row == 0), value, tile)
    return tile


def first_forward_kernel(n_rd, *refs):
    table, ids, info, obs, tiles = refs[:5]
    sent = refs[5 : 5 + n_rd]
    out, x0n, dampn, names, spread, tags, sems = refs[5 + n_rd :]
    slots = ids.shape[0]
    own = (sent[0].shape[0] - 1) // 2
    me = info[0]
    for k in range(n_rd):
        tags[k] = sent[k][2 * own].astype(I32)
    copy = pltpu.make_async_copy(tags, names, sems.at[0])
    copy.start()
    for k in range(n_rd):
        share = partner(me, k, n_rd)
        for j in range(SLOTS):
            slot = share * SLOTS + j
            local = jnp.maximum(ids[slot] - share * own, 0)
            x0n[slot] = sent[k][local]
            dampn[slot] = sent[k][own + local]
    out[...] = jnp.zeros(out.shape, F32)
    forward_tiles(table, info[2], tiles, x0n, spread, out)
    out[...] = -out[...]
    mine = obs.shape[0]
    start = info[1] * mine
    out[pl.ds(start, mine)] = out[pl.ds(start, mine)] + obs[...]
    copy.wait()


def row_kernel(n_pr, stage, *refs):
    table, info, tiles = refs[:3]
    shares = refs[3 : 3 + n_pr]
    rest = refs[3 + n_pr :]
    if stage == 2:
        image0, rest = rest[0], rest[1:]
    payload, image, wide = rest
    blocks = image.shape[0]
    slots = payload.shape[0] - 1
    summed = shares[0][0:blocks]
    for share in shares[1:]:
        summed = summed + share[0:blocks]
    image[...] = summed
    if stage > 0:
        scalars = shares[0][blocks]
        for share in shares[1:]:
            scalars = scalars + share[blocks]
        added = [0.0, total(summed * summed)]
        if stage == 2:
            added.append(total(summed * image0[...]))
        payload[slots] = scalars + scalar_tile(added)
    else:
        payload[slots] = jnp.zeros((ROWS, LANES), F32)
    adjoint_tiles(table, info[2], tiles, image, wide, payload)


def own_sums(me, names, sent, own, into):
    into[...] = jnp.zeros(into.shape, F32)
    for k in range(len(sent)):
        for j in range(SLOTS):
            slot = me * SLOTS + j
            local = jnp.maximum(names[k, 0, slot] - me * own, 0)
            into[local] += sent[k][slot]


def needed_sums(names, sent, slots):
    found = []
    for s in range(slots):
        tag = names[0, 0, s]
        value = sent[0][s]
        for k in range(1, len(sent)):
            for j in range(SLOTS):
                other = s // SLOTS * SLOTS + j
                value = value + jnp.where(names[k, 0, other] == tag, sent[k][other], 0.0)
        found.append(value)
    return jnp.stack(found)


def second_forward_kernel(n_rd, *refs):
    table, info, names, tiles, x0, damp, x0n, dampn = refs[:8]
    sent = refs[8 : 8 + n_rd]
    out, res, resn, spread = refs[8 + n_rd :]
    blocks = out.shape[0] - 1
    own = x0.shape[0]
    own_sums(info[0], names, sent, own, res)
    r = res[...] - damp[...] * x0[...]
    res[...] = r
    resn[...] = needed_sums(names, sent, resn.shape[0]) - dampn[...] * x0n[...]
    out[...] = jnp.zeros(out.shape, F32)
    out[blocks] = scalar_tile([total(r * r), total(damp[...] * r * r)])
    forward_tiles(table, info[2], tiles, resn, spread, out)


def column_scalars(sent, slots, many):
    summed = sent[0][slots]
    for other in sent[1:]:
        summed = summed + other[slots]
    return [summed[0:1, k : k + 1] for k in range(many)]


def third_forward_kernel(n_rd, *refs):
    table, info, names, tiles, x0, damp, dampn, res0, res0n = refs[:9]
    sent = refs[9 : 9 + n_rd]
    out, x1, res1, prod0, known, res1n, spread = refs[9 + n_rd :]
    blocks = out.shape[0] - 1
    slots = res0n.shape[0]
    own = x0.shape[0]
    r0 = res0[...]
    own_sums(info[0], names, sent, own, prod0)
    q0 = prod0[...] + damp[...] * r0
    norm, bending = column_scalars(sent, slots, 2)
    step = norm / bending
    prod0[...] = q0
    x1[...] = x0[...] + step * r0
    r1 = r0 - step * q0
    res1[...] = r1
    res1n[...] = res0n[...] - step * (needed_sums(names, sent, slots) + dampn[...] * res0n[...])
    known[0] = scalar_tile([norm, bending])
    out[...] = jnp.zeros(out.shape, F32)
    out[blocks] = scalar_tile([total(r1 * r1), total(damp[...] * r1 * r1), total(damp[...] * r1 * r0)])
    forward_tiles(table, info[2], tiles, res1n, spread, out)


def last_kernel(n_rd, *refs):
    info, names, damp, x1, res0, res1, prod0, known = refs[:8]
    sent = refs[8 : 8 + n_rd]
    x2, res2, sums = refs[8 + n_rd :]
    own = damp.shape[0]
    slots = sent[0].shape[0] - 1
    r1 = res1[...]
    own_sums(info[0], names, sent, own, sums)
    h1 = sums[...] + damp[...] * r1
    norm1, r1_a_r1, r1_a_r0 = column_scalars(sent, slots, 3)
    norm0 = known[0][0:1, 0:1]
    bending0 = known[0][0:1, 1:2]
    ratio = norm1 / norm0
    bending = r1_a_r1 + ratio * (2.0 * r1_a_r0 + ratio * bending0)
    step = norm1 / bending
    x2[...] = x1[...] + step * (r1 + ratio * res0[...])
    res2[...] = r1 - step * (h1 + ratio * prod0[...])


def partner(me, k, n):
    if n & (n - 1) == 0:
        return me ^ k
    return lax.rem(me + n - k, n)


def exchange(values, axis, n):
    got = [values]
    for k in range(1, n):
        if n & (n - 1) == 0:
            pairs = [(i, i ^ k) for i in range(n)]
        else:
            pairs = [(i, (i + k) % n) for i in range(n)]
        got.append(lax.ppermute(values, axis, pairs))
    return got


def body(n_rd, n_pr, reading_geo, prism_geo, observed, warm_start, damping, pair_blocks, pair_count):
    cap = pair_blocks.shape[2]
    pairs = pair_blocks.reshape(cap, 2).T
    own = warm_start.shape[0] // BLK
    rblk = reading_geo.shape[1] // BLK
    slots = n_rd * SLOTS
    shaped = lambda v: v.reshape(-1, ROWS, LANES)
    x0, damp, obs = shaped(warm_start), shaped(damping), shaped(observed)
    place = jnp.stack([lax.axis_index("rd"), lax.axis_index("pr")]).astype(I32)
    array = lambda *lead: VMEM((*lead, ROWS, LANES), F32)
    wide = VMEM((slots * GROUPS, 8, LANES), F32)
    dma = pltpu.SemaphoreType.DMA
    room = 5 + slots * GROUPS * 8 * LANES * 4 // MIB

    payload, table, ids, info = call(
        prep_kernel,
        "prep",
        room,
        [array(2 * own + 1), SMEM((2, cap), I32), SMEM((slots,), I32), SMEM((3,), I32)],
        [SMEM, SMEM, SMEM, pl.ANY, pl.ANY],
        [pairs, pair_count, place, x0, damp],
        [dma((2,))],
    )
    columns = exchange(payload, "rd", n_rd)
    (tiles,) = call(
        tiles_kernel,
        "tiles",
        room + slots * FEATURES * BLK * 4 // MIB,
        [VMEM((cap * GROUPS, 8, BLK), F32)],
        [SMEM, SMEM, SMEM, pl.ANY, pl.ANY],
        [table, ids, info, reading_geo, prism_geo],
        [
            VMEM((cap, 8, BLK), F32),
            VMEM((slots, 8, BLK), F32),
            wide,
            VMEM((slots, FEATURES, BLK), F32),
            dma((cap,)),
            dma((slots,)),
        ],
    )
    share, x0n, dampn, names = call(
        functools.partial(first_forward_kernel, n_rd),
        "first_forward",
        room,
        [array(rblk), array(slots), array(slots), SMEM((n_rd, ROWS, LANES), I32)],
        [SMEM] * 3 + [VMEM] * (2 + n_rd),
        [table, ids, info, obs, tiles, *columns],
        [wide, VMEM((n_rd, ROWS, LANES), I32), dma((1,))],
    )
    rows = exchange(share, "pr", n_pr)

    def row_stage(stage, rows, extra):
        keep = stage == 1
        return call(
            functools.partial(row_kernel, n_pr, stage),
            f"row_{stage}",
            room,
            [array(slots + 1)] + [array(rblk)] * keep,
            [SMEM] * 2 + [VMEM] * (1 + n_pr + len(extra)),
            [table, info, tiles, *rows, *extra],
            [array(rblk)] * (not keep) + [wide],
        )

    (sums,) = row_stage(0, rows, [])
    columns = exchange(sums, "rd", n_rd)
    share, res0, res0n = call(
        functools.partial(second_forward_kernel, n_rd),
        "second_forward",
        room,
        [array(rblk + 1), array(own), array(slots)],
        [SMEM] * 3 + [VMEM] * (5 + n_rd),
        [table, info, names, tiles, x0, damp, x0n, dampn, *columns],
        [wide],
    )
    rows = exchange(share, "pr", n_pr)
    sums, image0 = row_stage(1, rows, [])
    columns = exchange(sums, "rd", n_rd)
    share, x1, res1, prod0, known = call(
        functools.partial(third_forward_kernel, n_rd),
        "third_forward",
        room,
        [array(rblk + 1), array(own), array(own), array(own), array(1)],
        [SMEM] * 3 + [VMEM] * (6 + n_rd),
        [table, info, names, tiles, x0, damp, dampn, res0, res0n, *columns],
        [array(slots), wide],
    )
    rows = exchange(share, "pr", n_pr)
    (sums,) = row_stage(2, rows, [image0])
    columns = exchange(sums, "rd", n_rd)
    result = jax.ShapeDtypeStruct((own, ROWS, LANES), F32)
    x2, res2 = call(
        functools.partial(last_kernel, n_rd),
        "last",
        room,
        [result, result],
        [SMEM] * 2 + [VMEM] * (6 + n_rd),
        [info, names, damp, x1, res0, res1, prod0, known, *columns],
        [array(own)],
    )
    return x2.reshape(-1), res2.reshape(-1)


def solution(mesh):
    placed = (
        P(None, ("sector", "rd")),
        P(None, ("sector", "pr")),
        P(("sector", "rd", "pr")),
        P(("sector", "pr", "rd")),
        P(("sector", "pr", "rd")),
        P(("sector", "rd"), "pr", None, None),
        P(("sector", "rd"), "pr"),
    )
    return jax.shard_map(
        functools.partial(body, mesh.shape["rd"], mesh.shape["pr"]),
        mesh=mesh,
        in_specs=placed,
        out_specs=(P(("sector", "pr", "rd")), P(("sector", "pr", "rd"))),
        check_vma=False,
    )
```

```python
import functools

import jax
import jax.numpy as jnp
from jax import lax
from jax.experimental import pallas as pl
from jax.experimental.pallas import tpu as pltpu
from jax.sharding import PartitionSpec as P

BLK = 512
LANES = 128
ROWS = BLK // LANES
GROUPS = BLK // 8
SLOTS = 2
MIB = 1024 * 1024
FEATURES = 64

length_scale = 8.0**0.5

F32 = jnp.float32
BF16 = jnp.bfloat16
I32 = jnp.int32
VMEM = pltpu.VMEM
SMEM = pltpu.SMEM
HBM = pltpu.HBM


def call(kernel, name, room, outs, ins, args, scratch=()):
    return pl.pallas_call(
        kernel,
        name=name,
        out_shape=outs,
        in_specs=[pl.BlockSpec(memory_space=s) for s in ins],
        out_specs=[pl.BlockSpec(memory_space=getattr(o, "memory_space", VMEM)) for o in outs],
        scratch_shapes=scratch,
        compiler_params=pltpu.CompilerParams(vmem_limit_bytes=room * MIB),
    )(*args)


def lane_index(shape):
    return lax.broadcasted_iota(jnp.int32, shape, len(shape) - 1)


def each(count, spare, one):
    def two(i, carry):
        one(2 * i)
        one(jnp.where(2 * i + 1 < count, 2 * i + 1, spare))
        return carry

    lax.fori_loop(0, (count + 1) // 2, two, 0)


def over(n, one, carry=0):
    if n > 8:
        return lax.fori_loop(0, n, one, carry)
    for s in range(n):
        carry = one(s, carry)
    return carry


def split3(x):
    a = x.astype(BF16).astype(F32)
    b = (x - a).astype(BF16).astype(F32)
    return a, b, x - a - b


def total(values):
    return jnp.sum(jnp.sum(values, axis=0), keepdims=True)


def prep_kernel(pairs_in, count, place, x0, damp, payload, table, ids, info, pairs, sems):
    own = x0.shape[0]
    slots = ids.shape[0]
    copies = [
        pltpu.make_async_copy(x0, payload.at[pl.ds(0, own)], sems.at[0]),
        pltpu.make_async_copy(damp, payload.at[pl.ds(own, own)], sems.at[1]),
    ]
    pairs_copy = pltpu.make_async_copy(pairs_in, pairs, sems.at[2])
    for copy in [pairs_copy, *copies]:
        copy.start()
    for s in range(slots):
        ids[s] = -1
    info[0] = place[0]
    info[1] = place[1]
    pairs_copy.wait()
    info[2] = count[0, 0]

    def assign(i, carry):
        block = pairs[1, i]
        share = block // own
        held = ids[share * SLOTS]
        here = jnp.logical_or(held < 0, held == block)
        slot = share * SLOTS + jnp.where(here, 0, 1)
        ids[slot] = block
        table[0, i] = pairs[0, i]
        table[1, i] = slot
        return carry

    lax.fori_loop(0, count[0, 0], assign, 0)
    table[0, pairs.shape[1]] = 0
    table[1, pairs.shape[1]] = 0
    payload[2 * own] = scalar_tile([ids[s].astype(F32) for s in range(slots)])
    for copy in copies:
        copy.wait()


def scaled(geo):
    row = lax.broadcasted_iota(I32, geo.shape, 0)
    return (geo - jnp.where(row < 2, 5.0, 0.0)) * length_scale


def features(geo, reading):
    row = lax.broadcasted_iota(I32, geo.shape, 0)
    norm = split3(jnp.broadcast_to(jnp.sum(geo * geo, axis=0, keepdims=True), geo.shape))
    last = jnp.where(row < 6, 1.0, 0.0)
    for k in range(3):
        last = jnp.where(row == (k if reading else 3 + k), norm[k], last)
    if reading:
        a, b, c = split3(geo * jnp.where(row < 2, -2.0, 2.0))
        blocks = [a, a, b, b, a, c, last]
    else:
        a, b, c = split3(geo)
        blocks = [a, b, a, b, c, a, last]
    blocks += [jnp.zeros_like(geo)] * (FEATURES // 8 - len(blocks))
    return jnp.concatenate(blocks, axis=0).astype(BF16)


def tiles_kernel(table, ids, info, readings, prisms, tiles, rgeo, pgeo, depth, feats, rsems, psems):
    slots = ids.shape[0]
    count = info[2]

    def reading_copy(i):
        start = pl.multiple_of(table[0, i] * BLK, BLK)
        return pltpu.make_async_copy(readings.at[:, pl.ds(start, BLK)], rgeo.at[i, pl.ds(0, 3)], rsems.at[i])

    def prism_copy(s):
        start = pl.multiple_of(jnp.maximum(ids[s], 0) * BLK, BLK)
        return pltpu.make_async_copy(prisms.at[:, pl.ds(start, BLK)], pgeo.at[s, pl.ds(0, 3)], psems.at[s])

    rgeo[...] = jnp.zeros(rgeo.shape, F32)
    pgeo[...] = jnp.zeros(pgeo.shape, F32)
    for s in range(slots):
        prism_copy(s).start()
    lax.fori_loop(0, count, lambda i, c: (reading_copy(i).start(), c)[1], 0)

    def prepare(s, carry):
        prism_copy(s).wait()
        geo = scaled(pgeo[s])
        feats[s] = features(geo, False).astype(F32)
        for q in range(ROWS):
            turned = geo[:, q * LANES : (q + 1) * LANES].T
            for g in range(GROUPS // ROWS):
                depth[s * GROUPS + q * (GROUPS // ROWS) + g] = jnp.broadcast_to(
                    turned[8 * g : 8 * g + 8, 2:3], (8, LANES)
                )
        return carry

    over(slots, prepare)
    lax.fori_loop(0, count, lambda i, c: (reading_copy(i).wait(), c)[1], 0)

    def one(i):
        s = table[1, i]
        geo = scaled(rgeo[i])
        mine = features(geo, True)
        theirs = feats[s].astype(BF16)
        tile = tiles.at[pl.ds(i * GROUPS, GROUPS)]
        depths = depth.at[pl.ds(s * GROUPS, GROUPS)]
        height = [jnp.broadcast_to(geo[2:3, c * LANES : (c + 1) * LANES], (8, LANES)) for c in range(ROWS)]
        for q in range(ROWS):
            squared = lax.dot_general(
                theirs[:, q * LANES : (q + 1) * LANES], mine, (((0,), (0,)), ((), ())), preferred_element_type=F32
            )
            for g in range(GROUPS // ROWS):
                v = q * (GROUPS // ROWS) + g
                up = depths[v]
                for c in range(ROWS):
                    w = height[c] + up
                    inv = lax.rsqrt(squared[8 * g : 8 * g + 8, c * LANES : (c + 1) * LANES])
                    tile[v, :, c * LANES : (c + 1) * LANES] = (w * inv) * (inv * inv)

    def two(i, carry):
        one(2 * i)
        one(jnp.minimum(2 * i + 1, count - 1))
        return carry

    lax.fori_loop(0, (count + 1) // 2, two, 0)

    @pl.when(count % 2 == 1)
    def _():
        spare = tiles.at[pl.ds(tiles.shape[0] - GROUPS, GROUPS)]
        spare[...] = jnp.zeros(spare.shape, F32)


def spread_lanes(need, spread):
    slots = need.shape[0]
    values = need[...].reshape(slots * ROWS, LANES)
    left = jnp.concatenate(split3(values), axis=0).astype(BF16)
    shape = (3 * slots * ROWS, ROWS * LANES)
    row = lax.broadcasted_iota(I32, shape, 0) % (slots * ROWS)
    part = lax.broadcasted_iota(I32, shape, 1) // LANES

    def one(s, carry):
        pick = jnp.where(row == ROWS * s + part, 1.0, 0.0).astype(BF16)
        got = lax.dot_general(left, pick, (((0,), (0,)), ((), ())), preferred_element_type=F32)
        for q in range(ROWS):
            for g in range(GROUPS // ROWS):
                spread[s * GROUPS + q * (GROUPS // ROWS) + g] = got[8 * g : 8 * g + 8, q * LANES : (q + 1) * LANES]
        return carry

    over(slots, one)


def forward_tiles(table, count, tiles, need, spread, out):
    spread_lanes(need, spread)

    def one(i):
        a = table[0, i]
        s = table[1, i]
        tile = tiles.at[pl.ds(i * GROUPS, GROUPS)]
        column = spread.at[pl.ds(s * GROUPS, GROUPS)]
        sums = [[jnp.zeros((8, LANES), F32) for _ in range(ROWS)] for _ in range(2)]
        for v in range(GROUPS):
            values = column[v]
            for c in range(ROWS):
                sums[v % 2][c] += tile[v, :, c * LANES : (c + 1) * LANES] * values
        added = [jnp.sum(sums[0][c] + sums[1][c], axis=0, keepdims=True) for c in range(ROWS)]
        out[a] += jnp.concatenate(added, axis=0)

    each(count, table.shape[1] - 1, one)


def adjoint_tiles(table, count, tiles, row, wide, out):
    slots = wide.shape[0] // GROUPS
    wide[...] = jnp.zeros(wide.shape, F32)

    def one(i):
        s = table[1, i]
        values = row[table[0, i]]
        spread = [jnp.broadcast_to(values[c : c + 1], (8, LANES)) for c in range(ROWS)]
        tile = tiles.at[pl.ds(i * GROUPS, GROUPS)]
        held = wide.at[pl.ds(s * GROUPS, GROUPS)]
        for v in range(GROUPS):
            t = [tile[v, :, c * LANES : (c + 1) * LANES] * spread[c] for c in range(ROWS)]
            held[v] += (t[0] + t[1]) + (t[2] + t[3])

    each(count, table.shape[1] - 1, one)
    lane = lane_index((8, LANES))

    def reduce(s, groups):
        groups = list(groups)
        for g in range(GROUPS // ROWS):
            for q in range(ROWS):
                added = jnp.sum(wide[s * GROUPS + q * (GROUPS // ROWS) + g], axis=1, keepdims=True)
                groups[g] = jnp.where(lane == ROWS * s + q, added, groups[g])
        return tuple(groups)

    groups = over(slots, reduce, (jnp.zeros((8, LANES), F32),) * (GROUPS // ROWS))
    flat = jnp.concatenate(groups, axis=0).T
    out[0:slots] = flat[0 : slots * ROWS].reshape(slots, ROWS, LANES)


def scalar_tile(values):
    lane = lane_index((ROWS, LANES))
    row = lax.broadcasted_iota(I32, (ROWS, LANES), 0)
    tile = jnp.zeros((ROWS, LANES), F32)
    for k, value in enumerate(values):
        tile = jnp.where(jnp.logical_and(lane == k, row == 0), value, tile)
    return tile


def first_forward_kernel(n_rd, *refs):
    table, ids, info, obs, tiles = refs[:5]
    sent = refs[5 : 5 + n_rd]
    out, x0n, dampn, names, spread, tags, sems = refs[5 + n_rd :]
    slots = ids.shape[0]
    own = (sent[0].shape[0] - 1) // 2
    me = info[0]
    for k in range(n_rd):
        tags[k] = sent[k][2 * own].astype(I32)
    copy = pltpu.make_async_copy(tags, names, sems.at[0])
    copy.start()
    for k in range(n_rd):
        share = partner(me, k, n_rd)
        for j in range(SLOTS):
            slot = share * SLOTS + j
            local = jnp.maximum(ids[slot] - share * own, 0)
            x0n[slot] = sent[k][local]
            dampn[slot] = sent[k][own + local]
    out[...] = jnp.zeros(out.shape, F32)
    forward_tiles(table, info[2], tiles, x0n, spread, out)
    out[...] = -out[...]
    mine = obs.shape[0]
    start = info[1] * mine
    out[pl.ds(start, mine)] = out[pl.ds(start, mine)] + obs[...]
    copy.wait()


def row_kernel(n_pr, stage, *refs):
    table, info, tiles = refs[:3]
    shares = refs[3 : 3 + n_pr]
    rest = refs[3 + n_pr :]
    if stage == 2:
        image0, rest = rest[0], rest[1:]
    payload, image, wide = rest
    blocks = image.shape[0]
    slots = payload.shape[0] - 1
    summed = shares[0][0:blocks]
    for share in shares[1:]:
        summed = summed + share[0:blocks]
    image[...] = summed
    if stage > 0:
        scalars = shares[0][blocks]
        for share in shares[1:]:
            scalars = scalars + share[blocks]
        added = [0.0, total(summed * summed)]
        if stage == 2:
            added.append(total(summed * image0[...]))
        payload[slots] = scalars + scalar_tile(added)
    else:
        payload[slots] = jnp.zeros((ROWS, LANES), F32)
    adjoint_tiles(table, info[2], tiles, image, wide, payload)


def own_sums(me, names, sent, own, into):
    into[...] = jnp.zeros(into.shape, F32)
    for k in range(len(sent)):
        for j in range(SLOTS):
            slot = me * SLOTS + j
            local = jnp.maximum(names[k, 0, slot] - me * own, 0)
            into[local] += sent[k][slot]


def needed_sums(names, sent, slots):
    found = []
    for s in range(slots):
        tag = names[0, 0, s]
        value = sent[0][s]
        for k in range(1, len(sent)):
            for j in range(SLOTS):
                other = s // SLOTS * SLOTS + j
                value = value + jnp.where(names[k, 0, other] == tag, sent[k][other], 0.0)
        found.append(value)
    return jnp.stack(found)


def second_forward_kernel(n_rd, *refs):
    table, info, names, tiles, x0, damp, x0n, dampn = refs[:8]
    sent = refs[8 : 8 + n_rd]
    out, res, resn, spread = refs[8 + n_rd :]
    blocks = out.shape[0] - 1
    own = x0.shape[0]
    own_sums(info[0], names, sent, own, res)
    r = res[...] - damp[...] * x0[...]
    res[...] = r
    resn[...] = needed_sums(names, sent, resn.shape[0]) - dampn[...] * x0n[...]
    out[...] = jnp.zeros(out.shape, F32)
    out[blocks] = scalar_tile([total(r * r), total(damp[...] * r * r)])
    forward_tiles(table, info[2], tiles, resn, spread, out)


def column_scalars(sent, slots, many):
    summed = sent[0][slots]
    for other in sent[1:]:
        summed = summed + other[slots]
    return [summed[0:1, k : k + 1] for k in range(many)]


def third_forward_kernel(n_rd, *refs):
    table, info, names, tiles, x0, damp, dampn, res0, res0n = refs[:9]
    sent = refs[9 : 9 + n_rd]
    out, x1, res1, prod0, known, res1n, spread = refs[9 + n_rd :]
    blocks = out.shape[0] - 1
    slots = res0n.shape[0]
    own = x0.shape[0]
    r0 = res0[...]
    own_sums(info[0], names, sent, own, prod0)
    q0 = prod0[...] + damp[...] * r0
    norm, bending = column_scalars(sent, slots, 2)
    step = norm / bending
    prod0[...] = q0
    x1[...] = x0[...] + step * r0
    r1 = r0 - step * q0
    res1[...] = r1
    res1n[...] = res0n[...] - step * (needed_sums(names, sent, slots) + dampn[...] * res0n[...])
    known[0] = scalar_tile([norm, bending])
    out[...] = jnp.zeros(out.shape, F32)
    out[blocks] = scalar_tile([total(r1 * r1), total(damp[...] * r1 * r1), total(damp[...] * r1 * r0)])
    forward_tiles(table, info[2], tiles, res1n, spread, out)


def last_kernel(n_rd, *refs):
    info, names, damp, x1, res0, res1, prod0, known = refs[:8]
    sent = refs[8 : 8 + n_rd]
    x2, res2, sums = refs[8 + n_rd :]
    own = damp.shape[0]
    slots = sent[0].shape[0] - 1
    r1 = res1[...]
    own_sums(info[0], names, sent, own, sums)
    h1 = sums[...] + damp[...] * r1
    norm1, r1_a_r1, r1_a_r0 = column_scalars(sent, slots, 3)
    norm0 = known[0][0:1, 0:1]
    bending0 = known[0][0:1, 1:2]
    ratio = norm1 / norm0
    bending = r1_a_r1 + ratio * (2.0 * r1_a_r0 + ratio * bending0)
    step = norm1 / bending
    x2[...] = x1[...] + step * (r1 + ratio * res0[...])
    res2[...] = r1 - step * (h1 + ratio * prod0[...])


def partner(me, k, n):
    if n & (n - 1) == 0:
        return me ^ k
    return lax.rem(me + n - k, n)


def exchange(values, axis, n):
    got = [values]
    for k in range(1, n):
        if n & (n - 1) == 0:
            pairs = [(i, i ^ k) for i in range(n)]
        else:
            pairs = [(i, (i + k) % n) for i in range(n)]
        got.append(lax.ppermute(values, axis, pairs))
    return got


def body(n_rd, n_pr, reading_geo, prism_geo, observed, warm_start, damping, pair_blocks, pair_count):
    cap = pair_blocks.shape[2]
    pairs = pair_blocks.reshape(cap, 2).T
    own = warm_start.shape[0] // BLK
    rblk = reading_geo.shape[1] // BLK
    slots = n_rd * SLOTS
    shaped = lambda v: v.reshape(-1, ROWS, LANES)
    x0, damp, obs = shaped(warm_start), shaped(damping), shaped(observed)
    place = jnp.stack([lax.axis_index("rd"), lax.axis_index("pr")]).astype(I32)
    array = lambda *lead: VMEM((*lead, ROWS, LANES), F32)
    wide = VMEM((slots * GROUPS, 8, LANES), F32)
    far = lambda v: pltpu.with_memory_space_constraint(v, HBM)
    dma = pltpu.SemaphoreType.DMA
    room = 5 + slots * GROUPS * 8 * LANES * 4 // MIB

    payload, table, ids, info = call(
        prep_kernel,
        "prep",
        room,
        [array(2 * own + 1), SMEM((2, cap + 1), I32), SMEM((slots,), I32), SMEM((3,), I32)],
        [HBM, SMEM, SMEM, HBM, HBM],
        [far(pairs), pair_count, place, far(x0), far(damp)],
        [SMEM((2, cap), I32), dma((3,))],
    )
    columns = exchange(payload, "rd", n_rd)
    (tiles,) = call(
        tiles_kernel,
        "tiles",
        room + slots * FEATURES * BLK * 4 // MIB,
        [VMEM(((cap + 1) * GROUPS, 8, BLK), F32)],
        [SMEM, SMEM, SMEM, HBM, HBM],
        [table, ids, info, far(reading_geo), far(prism_geo)],
        [
            VMEM((cap, 8, BLK), F32),
            VMEM((slots, 8, BLK), F32),
            wide,
            VMEM((slots, FEATURES, BLK), F32),
            dma((cap,)),
            dma((slots,)),
        ],
    )
    share, x0n, dampn, names = call(
        functools.partial(first_forward_kernel, n_rd),
        "first_forward",
        room,
        [array(rblk), array(slots), array(slots), SMEM((n_rd, ROWS, LANES), I32)],
        [SMEM] * 3 + [VMEM] * (2 + n_rd),
        [table, ids, info, obs, tiles, *columns],
        [wide, VMEM((n_rd, ROWS, LANES), I32), dma((1,))],
    )
    rows = exchange(share, "pr", n_pr)

    def row_stage(stage, rows, extra):
        keep = stage == 1
        return call(
            functools.partial(row_kernel, n_pr, stage),
            f"row_{stage}",
            room,
            [array(slots + 1)] + [array(rblk)] * keep,
            [SMEM] * 2 + [VMEM] * (1 + n_pr + len(extra)),
            [table, info, tiles, *rows, *extra],
            [array(rblk)] * (not keep) + [wide],
        )

    (sums,) = row_stage(0, rows, [])
    columns = exchange(sums, "rd", n_rd)
    share, res0, res0n = call(
        functools.partial(second_forward_kernel, n_rd),
        "second_forward",
        room,
        [array(rblk + 1), array(own), array(slots)],
        [SMEM] * 3 + [VMEM] * (5 + n_rd),
        [table, info, names, tiles, x0, damp, x0n, dampn, *columns],
        [wide],
    )
    rows = exchange(share, "pr", n_pr)
    sums, image0 = row_stage(1, rows, [])
    columns = exchange(sums, "rd", n_rd)
    share, x1, res1, prod0, known = call(
        functools.partial(third_forward_kernel, n_rd),
        "third_forward",
        room,
        [array(rblk + 1), array(own), array(own), array(own), array(1)],
        [SMEM] * 3 + [VMEM] * (6 + n_rd),
        [table, info, names, tiles, x0, damp, dampn, res0, res0n, *columns],
        [array(slots), wide],
    )
    rows = exchange(share, "pr", n_pr)
    (sums,) = row_stage(2, rows, [image0])
    columns = exchange(sums, "rd", n_rd)
    result = jax.ShapeDtypeStruct((own, ROWS, LANES), F32)
    x2, res2 = call(
        functools.partial(last_kernel, n_rd),
        "last",
        room,
        [result, result],
        [SMEM] * 2 + [VMEM] * (6 + n_rd),
        [info, names, damp, x1, res0, res1, prod0, known, *columns],
        [array(own)],
    )
    return x2.reshape(-1), res2.reshape(-1)


def solution(mesh):
    placed = (
        P(None, ("sector", "rd")),
        P(None, ("sector", "pr")),
        P(("sector", "rd", "pr")),
        P(("sector", "pr", "rd")),
        P(("sector", "pr", "rd")),
        P(("sector", "rd"), "pr", None, None),
        P(("sector", "rd"), "pr"),
    )
    return jax.shard_map(
        functools.partial(body, mesh.shape["rd"], mesh.shape["pr"]),
        mesh=mesh,
        in_specs=placed,
        out_specs=(P(("sector", "pr", "rd")), P(("sector", "pr", "rd"))),
        check_vma=False,
    )
```

```python
import functools

import jax
import jax.numpy as jnp
from jax import lax
from jax.experimental import pallas as pl
from jax.experimental.pallas import tpu as pltpu
from jax.sharding import PartitionSpec as P

BLK = 512
LANES = 128
ROWS = BLK // LANES
GROUPS = BLK // 8
SLOTS = 2
MIB = 1024 * 1024
FEATURES = 64

length_scale = 8.0**0.5

F32 = jnp.float32
BF16 = jnp.bfloat16
I32 = jnp.int32
VMEM = pltpu.VMEM
SMEM = pltpu.SMEM
HBM = pltpu.HBM


def call(kernel, name, room, outs, ins, args, scratch=()):
    return pl.pallas_call(
        kernel,
        name=name,
        out_shape=outs,
        in_specs=[pl.BlockSpec(memory_space=s) for s in ins],
        out_specs=[pl.BlockSpec(memory_space=getattr(o, "memory_space", VMEM)) for o in outs],
        scratch_shapes=scratch,
        compiler_params=pltpu.CompilerParams(vmem_limit_bytes=room * MIB),
    )(*args)


def lane_index(shape):
    return lax.broadcasted_iota(jnp.int32, shape, len(shape) - 1)


def each(count, spare, one):
    def two(i, carry):
        one(2 * i)
        one(jnp.where(2 * i + 1 < count, 2 * i + 1, spare))
        return carry

    lax.fori_loop(0, (count + 1) // 2, two, 0)


def over(n, one, carry=0):
    if n > 8:
        return lax.fori_loop(0, n, one, carry)
    for s in range(n):
        carry = one(s, carry)
    return carry


def split3(x):
    a = x.astype(BF16).astype(F32)
    b = (x - a).astype(BF16).astype(F32)
    return a, b, x - a - b


def total(values):
    return jnp.sum(jnp.sum(values, axis=0), keepdims=True)


def prep_kernel(pairs_in, place, x0, damp, payload, table, ids, info, pairs, sems):
    own = x0.shape[0]
    slots = ids.shape[0]
    copies = [
        pltpu.make_async_copy(x0, payload.at[pl.ds(0, own)], sems.at[0]),
        pltpu.make_async_copy(damp, payload.at[pl.ds(own, own)], sems.at[1]),
    ]
    pairs_copy = pltpu.make_async_copy(pairs_in, pairs, sems.at[2])
    for copy in [pairs_copy, *copies]:
        copy.start()
    for s in range(slots):
        ids[s] = -1
    info[0] = place[0]
    info[1] = place[1]
    pairs_copy.wait()
    info[2] = place[2]

    def assign(i, carry):
        block = pairs[1, i]
        share = block // own
        held = ids[share * SLOTS]
        here = jnp.logical_or(held < 0, held == block)
        slot = share * SLOTS + jnp.where(here, 0, 1)
        ids[slot] = block
        table[0, i] = pairs[0, i]
        table[1, i] = slot
        return carry

    lax.fori_loop(0, place[2], assign, 0)
    table[0, pairs.shape[1]] = 0
    table[1, pairs.shape[1]] = 0
    payload[2 * own] = scalar_tile([ids[s].astype(F32) for s in range(slots)])
    for copy in copies:
        copy.wait()


def scaled(geo):
    row = lax.broadcasted_iota(I32, geo.shape, 0)
    return (geo - jnp.where(row < 2, 5.0, 0.0)) * length_scale


def features(geo, reading):
    row = lax.broadcasted_iota(I32, geo.shape, 0)
    norm = split3(jnp.broadcast_to(jnp.sum(geo * geo, axis=0, keepdims=True), geo.shape))
    last = jnp.where(row < 6, 1.0, 0.0)
    for k in range(3):
        last = jnp.where(row == (k if reading else 3 + k), norm[k], last)
    if reading:
        a, b, c = split3(geo * jnp.where(row < 2, -2.0, 2.0))
        blocks = [a, a, b, b, a, c, last]
    else:
        a, b, c = split3(geo)
        blocks = [a, b, a, b, c, a, last]
    blocks += [jnp.zeros_like(geo)] * (FEATURES // 8 - len(blocks))
    return jnp.concatenate(blocks, axis=0).astype(BF16)


def tiles_kernel(table, ids, info, readings, prisms, tiles, rgeo, pgeo, ups, depth, feats, rsems, psems):
    slots = ids.shape[0]
    count = info[2]

    def reading_copy(i):
        start = pl.multiple_of(table[0, i] * BLK, BLK)
        return pltpu.make_async_copy(readings.at[:, pl.ds(start, BLK)], rgeo.at[i, pl.ds(0, 3)], rsems.at[i])

    def prism_copy(s):
        start = pl.multiple_of(jnp.maximum(ids[s], 0) * BLK, BLK)
        return pltpu.make_async_copy(prisms.at[:, pl.ds(start, BLK)], pgeo.at[s, pl.ds(0, 3)], psems.at[s])

    rgeo[...] = jnp.zeros(rgeo.shape, F32)
    pgeo[...] = jnp.zeros(pgeo.shape, F32)
    for s in range(slots):
        prism_copy(s).start()
    lax.fori_loop(0, count, lambda i, c: (reading_copy(i).start(), c)[1], 0)

    def prepare(s, carry):
        prism_copy(s).wait()
        geo = scaled(pgeo[s])
        feats[s] = features(geo, False).astype(F32)
        for q in range(ROWS):
            ups[s, q : q + 1] = geo[2:3, q * LANES : (q + 1) * LANES]
        return carry

    over(slots, prepare)
    spread_lanes(ups, depth)
    lax.fori_loop(0, count, lambda i, c: (reading_copy(i).wait(), c)[1], 0)

    def one(i):
        s = table[1, i]
        geo = scaled(rgeo[i])
        mine = features(geo, True)
        theirs = feats[s].astype(BF16)
        tile = tiles.at[pl.ds(i * GROUPS, GROUPS)]
        depths = depth.at[pl.ds(s * GROUPS, GROUPS)]
        height = [jnp.broadcast_to(geo[2:3, c * LANES : (c + 1) * LANES], (8, LANES)) for c in range(ROWS)]
        for q in range(ROWS):
            squared = lax.dot_general(
                theirs[:, q * LANES : (q + 1) * LANES], mine, (((0,), (0,)), ((), ())), preferred_element_type=F32
            )
            for g in range(GROUPS // ROWS):
                v = q * (GROUPS // ROWS) + g
                up = depths[v]
                for c in range(ROWS):
                    w = height[c] + up
                    inv = lax.rsqrt(squared[8 * g : 8 * g + 8, c * LANES : (c + 1) * LANES])
                    tile[v, :, c * LANES : (c + 1) * LANES] = (w * inv) * (inv * inv)

    def two(i, carry):
        one(2 * i)
        one(jnp.minimum(2 * i + 1, count - 1))
        return carry

    lax.fori_loop(0, (count + 1) // 2, two, 0)

    @pl.when(count % 2 == 1)
    def _():
        spare = tiles.at[pl.ds(tiles.shape[0] - GROUPS, GROUPS)]
        spare[...] = jnp.zeros(spare.shape, F32)


def spread_lanes(need, spread):
    slots = need.shape[0]
    values = need[...].reshape(slots * ROWS, LANES)
    left = jnp.concatenate(split3(values), axis=0).astype(BF16)
    shape = (3 * slots * ROWS, ROWS * LANES)
    row = lax.broadcasted_iota(I32, shape, 0) % (slots * ROWS)
    part = lax.broadcasted_iota(I32, shape, 1) // LANES

    def one(s, carry):
        pick = jnp.where(row == ROWS * s + part, 1.0, 0.0).astype(BF16)
        got = lax.dot_general(left, pick, (((0,), (0,)), ((), ())), preferred_element_type=F32)
        for q in range(ROWS):
            for g in range(GROUPS // ROWS):
                spread[s * GROUPS + q * (GROUPS // ROWS) + g] = got[8 * g : 8 * g + 8, q * LANES : (q + 1) * LANES]
        return carry

    over(slots, one)


def forward_tiles(table, count, tiles, need, spread, out):
    spread_lanes(need, spread)

    def one(i):
        a = table[0, i]
        s = table[1, i]
        tile = tiles.at[pl.ds(i * GROUPS, GROUPS)]
        column = spread.at[pl.ds(s * GROUPS, GROUPS)]
        sums = [[jnp.zeros((8, LANES), F32) for _ in range(ROWS)] for _ in range(2)]
        for v in range(GROUPS):
            values = column[v]
            for c in range(ROWS):
                sums[v % 2][c] += tile[v, :, c * LANES : (c + 1) * LANES] * values
        added = [jnp.sum(sums[0][c] + sums[1][c], axis=0, keepdims=True) for c in range(ROWS)]
        out[a] += jnp.concatenate(added, axis=0)

    each(count, table.shape[1] - 1, one)


def adjoint_tiles(table, count, tiles, row, wide, out):
    slots = wide.shape[0] // GROUPS
    wide[...] = jnp.zeros(wide.shape, F32)

    def one(i):
        s = table[1, i]
        values = row[table[0, i]]
        spread = [jnp.broadcast_to(values[c : c + 1], (8, LANES)) for c in range(ROWS)]
        tile = tiles.at[pl.ds(i * GROUPS, GROUPS)]
        held = wide.at[pl.ds(s * GROUPS, GROUPS)]
        for v in range(GROUPS):
            t = [tile[v, :, c * LANES : (c + 1) * LANES] * spread[c] for c in range(ROWS)]
            held[v] += (t[0] + t[1]) + (t[2] + t[3])

    each(count, table.shape[1] - 1, one)
    lane = lane_index((8, LANES))

    def reduce(s, groups):
        groups = list(groups)
        for g in range(GROUPS // ROWS):
            for q in range(ROWS):
                added = jnp.sum(wide[s * GROUPS + q * (GROUPS // ROWS) + g], axis=1, keepdims=True)
                groups[g] = jnp.where(lane == ROWS * s + q, added, groups[g])
        return tuple(groups)

    groups = over(slots, reduce, (jnp.zeros((8, LANES), F32),) * (GROUPS // ROWS))
    flat = jnp.concatenate(groups, axis=0).T
    out[0:slots] = flat[0 : slots * ROWS].reshape(slots, ROWS, LANES)


def scalar_tile(values):
    lane = lane_index((ROWS, LANES))
    row = lax.broadcasted_iota(I32, (ROWS, LANES), 0)
    tile = jnp.zeros((ROWS, LANES), F32)
    for k, value in enumerate(values):
        tile = jnp.where(jnp.logical_and(lane == k, row == 0), value, tile)
    return tile


def first_forward_kernel(n_rd, *refs):
    table, ids, info, obs, tiles = refs[:5]
    sent = refs[5 : 5 + n_rd]
    out, x0n, dampn, names, spread, tags, sems = refs[5 + n_rd :]
    slots = ids.shape[0]
    own = (sent[0].shape[0] - 1) // 2
    me = info[0]
    for k in range(n_rd):
        tags[k] = sent[k][2 * own].astype(I32)
    copy = pltpu.make_async_copy(tags, names, sems.at[0])
    copy.start()
    for k in range(n_rd):
        share = partner(me, k, n_rd)
        for j in range(SLOTS):
            slot = share * SLOTS + j
            local = jnp.maximum(ids[slot] - share * own, 0)
            x0n[slot] = sent[k][local]
            dampn[slot] = sent[k][own + local]
    out[...] = jnp.zeros(out.shape, F32)
    forward_tiles(table, info[2], tiles, x0n, spread, out)
    out[...] = -out[...]
    mine = obs.shape[0]
    start = info[1] * mine
    out[pl.ds(start, mine)] = out[pl.ds(start, mine)] + obs[...]
    copy.wait()


def row_kernel(n_pr, stage, *refs):
    table, info, tiles = refs[:3]
    shares = refs[3 : 3 + n_pr]
    rest = refs[3 + n_pr :]
    if stage == 2:
        image0, rest = rest[0], rest[1:]
    payload, image, wide = rest
    blocks = image.shape[0]
    slots = payload.shape[0] - 1
    summed = shares[0][0:blocks]
    for share in shares[1:]:
        summed = summed + share[0:blocks]
    image[...] = summed
    if stage > 0:
        scalars = shares[0][blocks]
        for share in shares[1:]:
            scalars = scalars + share[blocks]
        added = [0.0, total(summed * summed)]
        if stage == 2:
            added.append(total(summed * image0[...]))
        payload[slots] = scalars + scalar_tile(added)
    else:
        payload[slots] = jnp.zeros((ROWS, LANES), F32)
    adjoint_tiles(table, info[2], tiles, image, wide, payload)


def own_sums(me, names, sent, own, into):
    into[...] = jnp.zeros(into.shape, F32)
    for k in range(len(sent)):
        for j in range(SLOTS):
            slot = me * SLOTS + j
            local = jnp.maximum(names[k, 0, slot] - me * own, 0)
            into[local] += sent[k][slot]


def needed_sums(names, sent, slots):
    found = []
    for s in range(slots):
        tag = names[0, 0, s]
        value = sent[0][s]
        for k in range(1, len(sent)):
            for j in range(SLOTS):
                other = s // SLOTS * SLOTS + j
                value = value + jnp.where(names[k, 0, other] == tag, sent[k][other], 0.0)
        found.append(value)
    return jnp.stack(found)


def second_forward_kernel(n_rd, *refs):
    table, info, names, tiles, x0, damp, x0n, dampn = refs[:8]
    sent = refs[8 : 8 + n_rd]
    out, res, resn, spread = refs[8 + n_rd :]
    blocks = out.shape[0] - 1
    own = x0.shape[0]
    own_sums(info[0], names, sent, own, res)
    r = res[...] - damp[...] * x0[...]
    res[...] = r
    resn[...] = needed_sums(names, sent, resn.shape[0]) - dampn[...] * x0n[...]
    out[...] = jnp.zeros(out.shape, F32)
    out[blocks] = scalar_tile([total(r * r), total(damp[...] * r * r)])
    forward_tiles(table, info[2], tiles, resn, spread, out)


def column_scalars(sent, slots, many):
    summed = sent[0][slots]
    for other in sent[1:]:
        summed = summed + other[slots]
    return [summed[0:1, k : k + 1] for k in range(many)]


def third_forward_kernel(n_rd, *refs):
    table, info, names, tiles, x0, damp, dampn, res0, res0n = refs[:9]
    sent = refs[9 : 9 + n_rd]
    out, x1, res1, prod0, known, res1n, spread = refs[9 + n_rd :]
    blocks = out.shape[0] - 1
    slots = res0n.shape[0]
    own = x0.shape[0]
    r0 = res0[...]
    own_sums(info[0], names, sent, own, prod0)
    q0 = prod0[...] + damp[...] * r0
    norm, bending = column_scalars(sent, slots, 2)
    step = norm / bending
    prod0[...] = q0
    x1[...] = x0[...] + step * r0
    r1 = r0 - step * q0
    res1[...] = r1
    res1n[...] = res0n[...] - step * (needed_sums(names, sent, slots) + dampn[...] * res0n[...])
    known[0] = scalar_tile([norm, bending])
    out[...] = jnp.zeros(out.shape, F32)
    out[blocks] = scalar_tile([total(r1 * r1), total(damp[...] * r1 * r1), total(damp[...] * r1 * r0)])
    forward_tiles(table, info[2], tiles, res1n, spread, out)


def last_kernel(n_rd, *refs):
    info, names, damp, x1, res0, res1, prod0, known = refs[:8]
    sent = refs[8 : 8 + n_rd]
    x2, res2, sums = refs[8 + n_rd :]
    own = damp.shape[0]
    slots = sent[0].shape[0] - 1
    r1 = res1[...]
    own_sums(info[0], names, sent, own, sums)
    h1 = sums[...] + damp[...] * r1
    norm1, r1_a_r1, r1_a_r0 = column_scalars(sent, slots, 3)
    norm0 = known[0][0:1, 0:1]
    bending0 = known[0][0:1, 1:2]
    ratio = norm1 / norm0
    bending = r1_a_r1 + ratio * (2.0 * r1_a_r0 + ratio * bending0)
    step = norm1 / bending
    x2[...] = x1[...] + step * (r1 + ratio * res0[...])
    res2[...] = r1 - step * (h1 + ratio * prod0[...])


def partner(me, k, n):
    if n & (n - 1) == 0:
        return me ^ k
    return lax.rem(me + n - k, n)


def exchange(values, axis, n):
    got = [values]
    for k in range(1, n):
        if n & (n - 1) == 0:
            pairs = [(i, i ^ k) for i in range(n)]
        else:
            pairs = [(i, (i + k) % n) for i in range(n)]
        got.append(lax.ppermute(values, axis, pairs))
    return got


def body(n_rd, n_pr, reading_geo, prism_geo, observed, warm_start, damping, pair_blocks, pair_count):
    cap = pair_blocks.shape[2]
    pairs = pair_blocks.reshape(cap, 2).T
    own = warm_start.shape[0] // BLK
    rblk = reading_geo.shape[1] // BLK
    slots = n_rd * SLOTS
    shaped = lambda v: v.reshape(-1, ROWS, LANES)
    x0, damp, obs = shaped(warm_start), shaped(damping), shaped(observed)
    place = jnp.stack([lax.axis_index("rd"), lax.axis_index("pr"), pair_count[0, 0]]).astype(I32)
    array = lambda *lead: VMEM((*lead, ROWS, LANES), F32)
    wide = VMEM((slots * GROUPS, 8, LANES), F32)
    far = lambda v: pltpu.with_memory_space_constraint(v, HBM)
    dma = pltpu.SemaphoreType.DMA
    room = 5 + slots * GROUPS * 8 * LANES * 4 // MIB

    payload, table, ids, info = call(
        prep_kernel,
        "prep",
        room,
        [array(2 * own + 1), SMEM((2, cap + 1), I32), SMEM((slots,), I32), SMEM((3,), I32)],
        [HBM, SMEM, HBM, HBM],
        [far(pairs), place, far(x0), far(damp)],
        [SMEM((2, cap), I32), dma((3,))],
    )
    columns = exchange(payload, "rd", n_rd)
    (tiles,) = call(
        tiles_kernel,
        "tiles",
        room + slots * FEATURES * BLK * 4 // MIB,
        [VMEM(((cap + 1) * GROUPS, 8, BLK), F32)],
        [SMEM, SMEM, SMEM, HBM, HBM],
        [table, ids, info, far(reading_geo), far(prism_geo)],
        [
            VMEM((cap, 8, BLK), F32),
            VMEM((slots, 8, BLK), F32),
            array(slots),
            wide,
            VMEM((slots, FEATURES, BLK), F32),
            dma((cap,)),
            dma((slots,)),
        ],
    )
    share, x0n, dampn, names = call(
        functools.partial(first_forward_kernel, n_rd),
        "first_forward",
        room,
        [array(rblk), array(slots), array(slots), SMEM((n_rd, ROWS, LANES), I32)],
        [SMEM] * 3 + [VMEM] * (2 + n_rd),
        [table, ids, info, obs, tiles, *columns],
        [wide, VMEM((n_rd, ROWS, LANES), I32), dma((1,))],
    )
    rows = exchange(share, "pr", n_pr)

    def row_stage(stage, rows, extra):
        keep = stage == 1
        return call(
            functools.partial(row_kernel, n_pr, stage),
            f"row_{stage}",
            room,
            [array(slots + 1)] + [array(rblk)] * keep,
            [SMEM] * 2 + [VMEM] * (1 + n_pr + len(extra)),
            [table, info, tiles, *rows, *extra],
            [array(rblk)] * (not keep) + [wide],
        )

    (sums,) = row_stage(0, rows, [])
    columns = exchange(sums, "rd", n_rd)
    share, res0, res0n = call(
        functools.partial(second_forward_kernel, n_rd),
        "second_forward",
        room,
        [array(rblk + 1), array(own), array(slots)],
        [SMEM] * 3 + [VMEM] * (5 + n_rd),
        [table, info, names, tiles, x0, damp, x0n, dampn, *columns],
        [wide],
    )
    rows = exchange(share, "pr", n_pr)
    sums, image0 = row_stage(1, rows, [])
    columns = exchange(sums, "rd", n_rd)
    share, x1, res1, prod0, known = call(
        functools.partial(third_forward_kernel, n_rd),
        "third_forward",
        room,
        [array(rblk + 1), array(own), array(own), array(own), array(1)],
        [SMEM] * 3 + [VMEM] * (6 + n_rd),
        [table, info, names, tiles, x0, damp, dampn, res0, res0n, *columns],
        [array(slots), wide],
    )
    rows = exchange(share, "pr", n_pr)
    (sums,) = row_stage(2, rows, [image0])
    columns = exchange(sums, "rd", n_rd)
    result = jax.ShapeDtypeStruct((own, ROWS, LANES), F32)
    x2, res2 = call(
        functools.partial(last_kernel, n_rd),
        "last",
        room,
        [result, result],
        [SMEM] * 2 + [VMEM] * (6 + n_rd),
        [info, names, damp, x1, res0, res1, prod0, known, *columns],
        [array(own)],
    )
    return x2.reshape(-1), res2.reshape(-1)


def solution(mesh):
    placed = (
        P(None, ("sector", "rd")),
        P(None, ("sector", "pr")),
        P(("sector", "rd", "pr")),
        P(("sector", "pr", "rd")),
        P(("sector", "pr", "rd")),
        P(("sector", "rd"), "pr", None, None),
        P(("sector", "rd"), "pr"),
    )
    return jax.shard_map(
        functools.partial(body, mesh.shape["rd"], mesh.shape["pr"]),
        mesh=mesh,
        in_specs=placed,
        out_specs=(P(("sector", "pr", "rd")), P(("sector", "pr", "rd"))),
        check_vma=False,
    )
```
